32 devices in a mesh: row: 8 (over z, x), col: 4 (over y, core).
Axes of the slice: x: 2, y: 2, z: 4, core: 2. Of those that a mesh axis runs over, the one named last changes fastest.
Arguments:
- panel_transposed: float32 [256, 16384], P('col', 'row'), may hold values from -0.046875 to 0.046875
- trailing: float32 [16384, 2048], P('row', 'col'), may hold values from -6 to 6
Outputs:
- stop_factors: float32 [2048, 256], P('row')
- stop_blocks: float32 [2048, 2048], P('row', 'col')
- projected: float32 [16384, 2048], P('row', 'col')
The draws below stay inside these ranges and needn't reach their ends.
All inputs are finite; a program needn't handle non-finite values.
Results may differ from the reference program's by a relative error of at most 0.00026.
Values sent between devices are 32-bit elements; how exact they have to be, the bound alone decides.
A program may use at most 128 MiB of HBM per device.

```python
import jax
import jax.numpy as jnp
from jax import lax

NB = 256
ROWS_DEV = 2048
ROWS = 16384
NCOLS = 2048
N_ROW = 8


def levels(stream_key, extent, pieces, least, high):
    gain = 1.0
    for axis_at, shards_of in pieces:
        draws = jax.random.uniform(jax.random.fold_in(jax.random.fold_in(stream_key, 6), axis_at), (shards_of,), jnp.float32, least / len(pieces), high / len(pieces))
        gain = gain * jnp.repeat(jnp.exp(draws), extent[axis_at] // shards_of).reshape((-1,) + (1,) * (len(extent) - 1 - axis_at))
    return gain


def normal_values(own_key, extent, deviation, limit, shards=(), held_as=jnp.bfloat16):
    drawn = jax.random.normal(own_key, extent, jnp.float32) * deviation
    if len(shards) > 0:
        drawn = levels(own_key, extent, shards, -0.22, 0.18) * drawn
    return jnp.clip(drawn, min=-limit, max=limit).astype(held_as)


def setup_inputs(seed: int = 0) -> dict:
    keys = jax.random.split(jax.random.key(seed), 3)
    panel_transposed = normal_values(keys[0], (NB, ROWS), ROWS ** -0.5, 0.046875, ((0, 4), (1, 8)), jnp.float32)
    trailing = normal_values(keys[1], (ROWS, NCOLS), 1.0, 6.0, ((0, 8), (1, 4)), jnp.float32)
    return {"panel_transposed": panel_transposed, "trailing": trailing}


def reference(panel_transposed, trailing):
    highest = lax.Precision.HIGHEST
    panel_blocks = panel_transposed.reshape(NB, N_ROW, ROWS_DEV)
    trail_blocks = trailing.reshape(N_ROW, ROWS_DEV, NCOLS)
    grams = jnp.einsum('asr,bsr->sab', panel_blocks, panel_blocks, precision=highest)
    crosses = jnp.einsum('asr,src->sac', panel_blocks, trail_blocks, precision=highest)
    prefix_gram = jnp.cumsum(grams, axis=0)
    prefix_cross = jnp.cumsum(crosses, axis=0)
    lowers = jnp.linalg.cholesky(prefix_gram)
    stop_blocks = jax.scipy.linalg.solve_triangular(lowers, prefix_cross, lower=True)
    stop_factors = jnp.swapaxes(lowers, 1, 2).reshape(N_ROW * NB, NB)
    coeffs = jax.scipy.linalg.solve_triangular(lowers[-1].T, stop_blocks[-1], lower=False)
    projected = trailing - jnp.einsum('ar,ac->rc', panel_transposed, coeffs, precision=highest)
    return (stop_factors, stop_blocks.reshape(N_ROW * NB, NCOLS), projected)
```

```python
import functools

import jax
import jax.numpy as jnp
from jax import lax
from jax.experimental import pallas as pl
from jax.experimental.pallas import tpu as pltpu
from jax.sharding import PartitionSpec as P

F32 = jnp.float32
MESH = pl.DeviceIdType.MESH
BLOCK = 32
GROUP = 4
CHUNKS = 4


def dot(left, right, dims=((1,), (0,))):
    return lax.dot_general(
        left, right, (dims, ((), ())), precision=lax.Precision.HIGHEST, preferred_element_type=F32
    )


def factor_rows(at, width, read, works):
    first = at * BLOCK
    low = (first // 128) * 128
    high = width + min(width, ((first + BLOCK + 127) // 128) * 128)
    spans = list(range(low, high, 128))
    tall = BLOCK // 8
    deep = max(128, ((first + 127) // 128) * 128)
    sub = lax.broadcasted_iota(jnp.int32, (8, 128), 0)
    lane = lax.broadcasted_iota(jnp.int32, (8, 128), 1)
    states = []
    for which, work in enumerate(works):
        update = None
        if at > 0:
            side = work[0:deep, low : low + 128].T[first - low : first - low + BLOCK, :]
            update = dot(side, work[0:deep, low:high])
        rows = []
        for tile in range(tall):
            line = []
            for span in spans:
                row0 = first + tile * 8
                if span < width:
                    value = read(which, row0, span)
                else:
                    value = (sub + row0 == lane + (span - width)).astype(F32)
                if update is not None:
                    value = value - update[tile * 8 : tile * 8 + 8, span - low : span - low + 128]
                line.append(value)
            rows.append(line)
        states.append(rows)
    scales = [[jnp.zeros((8, 128), F32) for _ in range(tall)] for _ in works]
    for start in range(0, BLOCK, GROUP):
        top = start // 8
        spreads = []
        for rows in states:
            spreads.append(
                [
                    {
                        tile: jnp.broadcast_to(
                            rows[tile][0][:, first - low + start + k : first - low + start + k + 1],
                            (8, 128),
                        )
                        for tile in range(top, tall)
                    }
                    for k in range(GROUP)
                ]
            )
        for k in range(GROUP):
            place = (start + k) % 8
            for which, rows in enumerate(states):
                column = spreads[which][k]
                pivot = jnp.broadcast_to(column[top][place : place + 1, :], (8, 128))
                recip = 1.0 / pivot
                scales[which][top] = jnp.where(sub == place, lax.rsqrt(pivot), scales[which][top])
                factors = {tile: column[tile] * recip for tile in range(top, tall)}
                factors[top] = jnp.where(sub > place, factors[top], 0.0)
                for later in range(k + 1, GROUP):
                    other = spreads[which][later]
                    line = jnp.broadcast_to(other[top][place : place + 1, :], (8, 128))
                    for tile in range(top, tall):
                        other[tile] = other[tile] - factors[tile] * line
                for at_span in range(len(spans)):
                    line = jnp.broadcast_to(rows[top][at_span][place : place + 1, :], (8, 128))
                    for tile in range(top, tall):
                        rows[tile][at_span] = rows[tile][at_span] - factors[tile] * line
    for which, work in enumerate(works):
        for tile in range(tall):
            row0 = first + tile * 8
            for at_span, span in enumerate(spans):
                value = states[which][tile][at_span] * scales[which][tile]
                if span < width:
                    value = jnp.where(lane + span >= sub + row0, value, 0.0)
                work[row0 : row0 + 8, span : span + 128] = value


def flip(index, distance):
    return index + distance - 2 * distance * lax.rem(lax.div(index, distance), 2)


def chain_kernel(
    n_row, n_col, panel_ref, trailing_hbm, factors_ref, blocks_ref, coeffs_ref, whole_hbm,
    whole, tv, gsum, gpre, grecv, gfull, csum, cpre, crecv, work_own, work_last,
    local_sem, p_send, p_recv, f_send, f_recv, g_send, g_recv, c_send, c_recv,
    a_send, a_recv, b_send, b_recv,
):
    share, depth = panel_ref.shape
    width = share * n_col
    row, col = lax.axis_index("row"), lax.axis_index("col")
    steps = n_row.bit_length() - 1
    pairs = n_col // 2
    mate = flip(col, 1)
    ahead = [lax.rem(col + 2 * k, n_col) for k in range(1, pairs)]
    behind = [lax.rem(col + n_col - 2 * k, n_col) for k in range(1, pairs)]
    across = [flip(row, 2**h) for h in range(steps)]

    load = pltpu.make_async_copy(trailing_hbm, tv, local_sem.at[0])
    load.start()
    whole[col] = panel_ref[...]

    barrier = pltpu.get_barrier_semaphore()
    for target in [mate] + ahead:
        pl.semaphore_signal(barrier, inc=1, device_id=(row, target), device_id_type=MESH)
    for target in across:
        pl.semaphore_signal(barrier, inc=1, device_id=(target, col), device_id_type=MESH)
    pl.semaphore_wait(barrier, pairs + steps)

    def send(src, dst, send_sem, recv_sem, r, c):
        return pltpu.make_async_remote_copy(
            src_ref=src, dst_ref=dst, send_sem=send_sem, recv_sem=recv_sem,
            device_id=(r, c), device_id_type=MESH,
        )

    piece = depth // CHUNKS
    started = []
    direct = []
    for q in range(CHUNKS):
        cut = pl.ds(q * piece, piece)
        line = []
        for k, target in enumerate(ahead):
            copy = send(panel_ref.at[:, cut], whole.at[col, :, cut], p_send.at[k, q], p_recv.at[k, q], row, target)
            copy.start()
            line.append(copy)
        copy = send(panel_ref.at[:, cut], whole.at[col, :, cut], f_send.at[0, q], f_recv.at[0, q], row, mate)
        copy.start()
        direct.append((line, copy))
    load.wait()
    gram = None
    cross_started = []
    gram_copies = []
    cross_copies = []

    def gram_step(h):
        copy = send(gsum.at[h], grecv.at[h], g_send.at[h], g_recv.at[h], across[h], col)
        copy.start()
        gram_copies.append(copy)

    def gram_take(h):
        gram_copies[h].wait_recv()
        lower = across[h] < row
        gpre[...] = gpre[...] + jnp.where(lower, grecv[h], 0.0)
        gsum[h + 1] = gsum[h] + grecv[h]

    def cross_step(h):
        copy = send(csum.at[h], crecv.at[h], c_send.at[h], c_recv.at[h], across[h], col)
        copy.start()
        cross_copies.append(copy)

    def cross_take(h):
        cross_copies[h].wait_recv()
        lower = across[h] < row
        cpre[...] = cpre[...] + jnp.where(lower, crecv[h], 0.0)
        csum[h + 1] = csum[h] + crecv[h]

    for q in range(CHUNKS):
        cut = pl.ds(q * piece, piece)
        line, near = direct[q]
        forwards = []
        for k, copy in enumerate(line):
            copy.wait_recv()
            on = send(
                whole.at[behind[k], :, cut], whole.at[behind[k], :, cut],
                f_send.at[k + 1, q], f_recv.at[k + 1, q], row, mate,
            )
            on.start()
            forwards.append(on)
            started.append(copy)
        near.wait_recv()
        started.append(near)
        for on in forwards:
            on.wait_recv()
            started.append(on)
        part = whole[:, :, q * piece : (q + 1) * piece].reshape(width, piece)
        own = dot(panel_ref[:, q * piece : (q + 1) * piece], part, ((1,), (1,)))
        gram = own if gram is None else gram + own
        if q == CHUNKS - 1:
            gsum[0] = gram
            gpre[...] = gram
            gram_step(0)
        product = dot(part, tv[q * piece : (q + 1) * piece, :])
        if q == 0:
            csum[0] = product
        else:
            csum[0] = csum[0] + product
    cross_step(0)
    cpre[...] = csum[0]
    out = pltpu.make_async_copy(whole, whole_hbm, local_sem.at[1])
    out.start()
    work_own[...] = jnp.zeros_like(work_own)
    work_last[...] = jnp.zeros_like(work_last)
    for h in range(steps):
        gram_take(h)
        if h + 1 < steps:
            gram_step(h + 1)

    gfull[col, 0] = gpre[...]
    gfull[col, 1] = gsum[steps]
    far = []
    for k, target in enumerate(ahead):
        copy = send(gfull.at[col], gfull.at[col], a_send.at[k], a_recv.at[k], row, target)
        copy.start()
        far.append(copy)
    near = send(gfull.at[col], gfull.at[col], b_send.at[0], b_recv.at[0], row, mate)
    near.start()
    forwards = []
    for k, copy in enumerate(far):
        copy.wait_recv()
        on = send(gfull.at[behind[k]], gfull.at[behind[k]], b_send.at[k + 1], b_recv.at[k + 1], row, mate)
        on.start()
        forwards.append(on)
    near.wait_recv()
    for on in forwards:
        on.wait_recv()

    def read(which, row0, span):
        return gfull[row0 // share, which, row0 % share : row0 % share + 8, span : span + 128]

    count = width // BLOCK
    done = 0
    for at in range(count):
        factor_rows(at, width, read, (work_own, work_last))
        while done < steps and (done + 1) * count <= (at + 1) * steps:
            cross_take(done)
            done += 1
            if done < steps:
                cross_step(done)
    factors_ref[...] = work_own[:, :width]
    middle = dot(work_last[:, width:], csum[steps])
    coeffs_ref[...] = dot(work_last[:, width:], middle, ((0,), (0,)))
    blocks_ref[...] = dot(work_own[:, width:], cpre[...])
    out.wait()
    for copy in started + gram_copies + cross_copies + far + [near] + forwards:
        copy.wait_send()


def chain(panel, trailing, n_row, n_col):
    share, depth = panel.shape
    width = share * n_col
    cols = trailing.shape[1]
    steps = n_row.bit_length() - 1
    pairs = n_col // 2
    dma = pltpu.SemaphoreType.DMA
    vmem = pl.BlockSpec(memory_space=pltpu.VMEM)
    hbm = pl.BlockSpec(memory_space=pl.ANY)
    apart = max(pairs - 1, 1)
    return pl.pallas_call(
        functools.partial(chain_kernel, n_row, n_col),
        out_shape=(
            jax.ShapeDtypeStruct((width, width), F32),
            jax.ShapeDtypeStruct((width, cols), F32),
            jax.ShapeDtypeStruct((width, cols), F32),
            jax.ShapeDtypeStruct((n_col, share, depth), F32),
        ),
        in_specs=[vmem, hbm],
        out_specs=(vmem, vmem, vmem, hbm),
        scratch_shapes=[
            pltpu.VMEM((n_col, share, depth), F32),
            pltpu.VMEM((depth, cols), F32),
            pltpu.VMEM((steps + 1, share, width), F32),
            pltpu.VMEM((share, width), F32),
            pltpu.VMEM((steps, share, width), F32),
            pltpu.VMEM((n_col, 2, share, width), F32),
            pltpu.VMEM((steps + 1, width, cols), F32),
            pltpu.VMEM((width, cols), F32),
            pltpu.VMEM((steps, width, cols), F32),
            pltpu.VMEM((width, 2 * width), F32),
            pltpu.VMEM((width, 2 * width), F32),
            dma((2,)),
            dma((apart, CHUNKS)),
            dma((apart, CHUNKS)),
            dma((pairs, CHUNKS)),
            dma((pairs, CHUNKS)),
            dma((steps,)),
            dma((steps,)),
            dma((steps,)),
            dma((steps,)),
            dma((apart,)),
            dma((apart,)),
            dma((pairs,)),
            dma((pairs,)),
        ],
        compiler_params=pltpu.CompilerParams(
            collective_id=0, has_side_effects=True, vmem_limit_bytes=44 * 2**20
        ),
    )(panel, trailing)


def remove_kernel(whole_ref, coeffs_ref, trailing_ref, out_ref):
    part = whole_ref[...].reshape(coeffs_ref.shape[0], whole_ref.shape[2])
    out_ref[...] = trailing_ref[...] - dot(part, coeffs_ref[...], ((0,), (0,)))


def remove(whole, coeffs, trailing):
    depth, cols = trailing.shape
    n_col, share, _ = whole.shape
    tile = depth // 4
    return pl.pallas_call(
        remove_kernel,
        grid=(depth // tile,),
        out_shape=jax.ShapeDtypeStruct((depth, cols), F32),
        in_specs=[
            pl.BlockSpec((n_col, share, tile), lambda i: (0, 0, i)),
            pl.BlockSpec(coeffs.shape, lambda i: (0, 0)),
            pl.BlockSpec((tile, cols), lambda i: (i, 0)),
        ],
        out_specs=pl.BlockSpec((tile, cols), lambda i: (i, 0)),
        compiler_params=pltpu.CompilerParams(vmem_limit_bytes=32 * 2**20),
    )(whole, coeffs, trailing)


def solution(mesh):
    n_row, n_col = mesh.shape["row"], mesh.shape["col"]

    def shards(panel, trailing):
        factors, blocks, coeffs, whole = chain(panel, trailing, n_row, n_col)
        return factors, blocks, remove(whole, coeffs, trailing)

    return jax.shard_map(
        shards,
        mesh=mesh,
        in_specs=(P("col", "row"), P("row", "col")),
        out_specs=(P("row", None), P("row", "col"), P("row", "col")),
        check_vma=False,
    )
```

```python
import functools

import jax
import jax.numpy as jnp
from jax import lax
from jax.experimental import pallas as pl
from jax.experimental.pallas import tpu as pltpu
from jax.sharding import PartitionSpec as P

F32 = jnp.float32
MESH = pl.DeviceIdType.MESH
BLOCK = 32
GROUP = 8
CHUNKS = 4


def dot(left, right, dims=((1,), (0,))):
    return lax.dot_general(
        left, right, (dims, ((), ())), precision=lax.Precision.HIGHEST, preferred_element_type=F32
    )


def factor_rows(at, width, read, works):
    first = at * BLOCK
    low = (first // 128) * 128
    high = width + min(width, ((first + BLOCK + 127) // 128) * 128)
    spans = list(range(low, high, 128))
    tall = BLOCK // 8
    deep = max(128, ((first + 127) // 128) * 128)
    sub = lax.broadcasted_iota(jnp.int32, (8, 128), 0)
    lane = lax.broadcasted_iota(jnp.int32, (8, 128), 1)
    states = []
    for which, work in enumerate(works):
        update = None
        if at > 0:
            side = work[0:deep, low : low + 128].T[first - low : first - low + BLOCK, :]
            update = dot(side, work[0:deep, low:high])
        rows = []
        for tile in range(tall):
            line = []
            for span in spans:
                row0 = first + tile * 8
                if span < width:
                    value = read(which, row0, span)
                else:
                    value = (sub + row0 == lane + (span - width)).astype(F32)
                if update is not None:
                    value = value - update[tile * 8 : tile * 8 + 8, span - low : span - low + 128]
                line.append(value)
            rows.append(line)
        states.append(rows)
    scales = [[jnp.zeros((8, 128), F32) for _ in range(tall)] for _ in works]
    for start in range(0, BLOCK, GROUP):
        top = start // 8
        spreads = []
        for rows in states:
            spreads.append(
                [
                    {
                        tile: jnp.broadcast_to(
                            rows[tile][0][:, first - low + start + k : first - low + start + k + 1],
                            (8, 128),
                        )
                        for tile in range(top, tall)
                    }
                    for k in range(GROUP)
                ]
            )
        for k in range(GROUP):
            place = (start + k) % 8
            for which, rows in enumerate(states):
                column = spreads[which][k]
                pivot = jnp.broadcast_to(column[top][place : place + 1, :], (8, 128))
                recip = 1.0 / pivot
                scales[which][top] = jnp.where(sub == place, lax.rsqrt(pivot), scales[which][top])
                factors = {tile: column[tile] * recip for tile in range(top, tall)}
                factors[top] = jnp.where(sub > place, factors[top], 0.0)
                for later in range(k + 1, GROUP):
                    other = spreads[which][later]
                    line = jnp.broadcast_to(other[top][place : place + 1, :], (8, 128))
                    for tile in range(top, tall):
                        other[tile] = other[tile] - factors[tile] * line
                for at_span in range(len(spans)):
                    line = jnp.broadcast_to(rows[top][at_span][place : place + 1, :], (8, 128))
                    for tile in range(top, tall):
                        rows[tile][at_span] = rows[tile][at_span] - factors[tile] * line
    for which, work in enumerate(works):
        for tile in range(tall):
            row0 = first + tile * 8
            for at_span, span in enumerate(spans):
                value = states[which][tile][at_span] * scales[which][tile]
                if span < width:
                    value = jnp.where(lane + span >= sub + row0, value, 0.0)
                work[row0 : row0 + 8, span : span + 128] = value


def flip(index, distance):
    return index + distance - 2 * distance * lax.rem(lax.div(index, distance), 2)


def chain_kernel(
    n_row, n_col, panel_hbm, trailing_hbm, factors_ref, blocks_ref, coeffs_ref, whole_hbm,
    whole, tv, gsum, gpre, grecv, gfull, csum, cpre, crecv, ctotal, cprefix, work_own, work_last,
    local_sem, p_send, p_recv, f_send, f_recv, g_send, g_recv, c_send, c_recv,
    a_send, a_recv, b_send, b_recv,
):
    share, depth = panel_hbm.shape
    width = share * n_col
    cols = tv.shape[1]
    row, col = lax.axis_index("row"), lax.axis_index("col")
    steps = n_row.bit_length() - 1
    pairs = n_col // 2
    mate = flip(col, 1)
    ahead = [lax.rem(col + 2 * k, n_col) for k in range(1, pairs)]
    behind = [lax.rem(col + n_col - 2 * k, n_col) for k in range(1, pairs)]
    across = [flip(row, 2**h) for h in range(steps)]
    order = [col, mate]
    for source in behind:
        order += [source, flip(source, 1)]

    own_load = pltpu.make_async_copy(panel_hbm, whole.at[col], local_sem.at[2])
    own_load.start()
    load = pltpu.make_async_copy(trailing_hbm, tv, local_sem.at[0])
    load.start()

    barrier = pltpu.get_barrier_semaphore()
    for target in [mate] + ahead:
        pl.semaphore_signal(barrier, inc=1, device_id=(row, target), device_id_type=MESH)
    for target in across:
        pl.semaphore_signal(barrier, inc=1, device_id=(target, col), device_id_type=MESH)
    work_own[...] = jnp.zeros_like(work_own)
    work_last[...] = jnp.zeros_like(work_last)
    pl.semaphore_wait(barrier, pairs + steps)

    def send(src, dst, send_sem, recv_sem, r, c):
        return pltpu.make_async_remote_copy(
            src_ref=src, dst_ref=dst, send_sem=send_sem, recv_sem=recv_sem,
            device_id=(r, c), device_id_type=MESH,
        )

    piece = depth // CHUNKS
    own_load.wait()
    started = []
    direct = []
    for q in range(CHUNKS):
        cut = pl.ds(q * piece, piece)
        line = []
        for k, target in enumerate(ahead):
            copy = send(whole.at[col, :, cut], whole.at[col, :, cut], p_send.at[k, q], p_recv.at[k, q], row, target)
            copy.start()
            line.append(copy)
        copy = send(whole.at[col, :, cut], whole.at[col, :, cut], f_send.at[0, q], f_recv.at[0, q], row, mate)
        copy.start()
        direct.append((line, copy))
    gram = None
    gram_copies = []
    cross_copies = {}

    def gram_step(h):
        copy = send(gsum.at[h], grecv.at[h], g_send.at[h], g_recv.at[h], across[h], col)
        copy.start()
        gram_copies.append(copy)

    def gram_take(h):
        gram_copies[h].wait_recv()
        lower = across[h] < row
        gpre[...] = gpre[...] + jnp.where(lower, grecv[h], 0.0)
        gsum[h + 1] = gsum[h] + grecv[h]

    def cross_step(at, h):
        copy = send(csum.at[h, at], crecv.at[h, at], c_send.at[h, at], c_recv.at[h, at], across[h], col)
        copy.start()
        cross_copies[at, h] = copy

    def cross_take(at, h):
        cross_copies[at, h].wait_recv()
        lower = across[h] < row
        before = cpre[at] + jnp.where(lower, crecv[h, at], 0.0)
        total = csum[h, at] + crecv[h, at]
        if h + 1 < steps:
            cpre[at] = before
            csum[h + 1, at] = total
            cross_step(at, h + 1)
        else:
            cprefix[order[at]] = before
            ctotal[order[at]] = total

    def cross_start(pair):
        slices = [whole[order[2 * pair]], whole[order[2 * pair + 1]]]
        both = dot(jnp.concatenate(slices, 0), tv[...])
        for half, at in enumerate((2 * pair, 2 * pair + 1)):
            own = both[half * share : (half + 1) * share]
            csum[0, at] = own
            cpre[at] = own
            cross_step(at, 0)

    load.wait()
    for _, near in direct:
        near.wait_recv()
        started.append(near)
    cross_start(0)
    for q in range(CHUNKS):
        cut = pl.ds(q * piece, piece)
        forwards = []
        for k, copy in enumerate(direct[q][0]):
            copy.wait_recv()
            on = send(
                whole.at[behind[k], :, cut], whole.at[behind[k], :, cut],
                f_send.at[k + 1, q], f_recv.at[k + 1, q], row, mate,
            )
            on.start()
            forwards.append(on)
            started.append(copy)
        if q == 1:
            cross_take(0, 0)
            cross_take(1, 0)
        for on in forwards:
            on.wait_recv()
            started.append(on)
        part = whole[:, :, q * piece : (q + 1) * piece].reshape(width, piece)
        own = dot(whole[col, :, q * piece : (q + 1) * piece], part, ((1,), (1,)))
        gram = own if gram is None else gram + own
    gsum[0] = gram
    gpre[...] = gram
    gram_step(0)
    out = pltpu.make_async_copy(whole, whole_hbm, local_sem.at[1])
    out.start()
    for pair in range(1, pairs):
        cross_start(pair)
    for h in range(steps):
        gram_take(h)
        if h + 1 < steps:
            gram_step(h + 1)

    gfull[col, 0] = gpre[...]
    gfull[col, 1] = gsum[steps]
    far = []
    for k, target in enumerate(ahead):
        copy = send(gfull.at[col], gfull.at[col], a_send.at[k], a_recv.at[k], row, target)
        copy.start()
        far.append(copy)
    near = send(gfull.at[col], gfull.at[col], b_send.at[0], b_recv.at[0], row, mate)
    near.start()
    pending = [(at, h) for h in range(1, steps) for at in (0, 1)]
    late = [(at, h) for h in range(steps) for at in range(2, n_col)]
    if steps > 1:
        for at in (0, 1):
            cross_take(*pending.pop(0))
    for _ in range(n_col - 2):
        cross_take(*late.pop(0))
    forwards = []
    for k, copy in enumerate(far):
        copy.wait_recv()
        on = send(gfull.at[behind[k]], gfull.at[behind[k]], b_send.at[k + 1], b_recv.at[k + 1], row, mate)
        on.start()
        forwards.append(on)
    near.wait_recv()
    for on in forwards:
        on.wait_recv()

    def read(which, row0, span):
        return gfull[row0 // share, which, row0 % share : row0 % share + 8, span : span + 128]

    count = width // BLOCK
    rest = sorted(pending + late, key=lambda turn: (turn[1], turn[0]))
    held = len(rest)
    for at in range(count):
        factor_rows(at, width, read, (work_own, work_last))
        while rest and (held - len(rest) + 1) * count <= (at + 1) * held:
            cross_take(*rest.pop(0))
    factors_ref[...] = work_own[:, :width]
    middle = dot(work_last[:, width:], ctotal[...].reshape(width, cols))
    coeffs_ref[...] = dot(work_last[:, width:], middle, ((0,), (0,)))
    blocks_ref[...] = dot(work_own[:, width:], cprefix[...].reshape(width, cols))
    out.wait()
    for copy in started + gram_copies + list(cross_copies.values()) + far + [near] + forwards:
        copy.wait_send()


def chain(panel, trailing, n_row, n_col):
    share, depth = panel.shape
    width = share * n_col
    cols = trailing.shape[1]
    steps = n_row.bit_length() - 1
    pairs = n_col // 2
    dma = pltpu.SemaphoreType.DMA
    vmem = pl.BlockSpec(memory_space=pltpu.VMEM)
    hbm = pl.BlockSpec(memory_space=pl.ANY)
    apart = max(pairs - 1, 1)
    return pl.pallas_call(
        functools.partial(chain_kernel, n_row, n_col),
        out_shape=(
            jax.ShapeDtypeStruct((width, width), F32),
            jax.ShapeDtypeStruct((width, cols), F32),
            jax.ShapeDtypeStruct((width, cols), F32),
            jax.ShapeDtypeStruct((n_col, share, depth), F32),
        ),
        in_specs=[hbm, hbm],
        out_specs=(vmem, vmem, vmem, hbm),
        scratch_shapes=[
            pltpu.VMEM((n_col, share, depth), F32),
            pltpu.VMEM((depth, cols), F32),
            pltpu.VMEM((steps + 1, share, width), F32),
            pltpu.VMEM((share, width), F32),
            pltpu.VMEM((steps, share, width), F32),
            pltpu.VMEM((n_col, 2, share, width), F32),
            pltpu.VMEM((steps, n_col, share, cols), F32),
            pltpu.VMEM((n_col, share, cols), F32),
            pltpu.VMEM((steps, n_col, share, cols), F32),
            pltpu.VMEM((n_col, share, cols), F32),
            pltpu.VMEM((n_col, share, cols), F32),
            pltpu.VMEM((width, 2 * width), F32),
            pltpu.VMEM((width, 2 * width), F32),
            dma((3,)),
            dma((apart, CHUNKS)),
            dma((apart, CHUNKS)),
            dma((pairs, CHUNKS)),
            dma((pairs, CHUNKS)),
            dma((steps,)),
            dma((steps,)),
            dma((steps, n_col)),
            dma((steps, n_col)),
            dma((apart,)),
            dma((apart,)),
            dma((pairs,)),
            dma((pairs,)),
        ],
        compiler_params=pltpu.CompilerParams(
            collective_id=0, has_side_effects=True, vmem_limit_bytes=56 * 2**20
        ),
    )(panel, trailing)


def remove_kernel(whole_ref, coeffs_ref, trailing_ref, out_ref):
    part = whole_ref[...].reshape(coeffs_ref.shape[0], whole_ref.shape[2])
    out_ref[...] = trailing_ref[...] - dot(part, coeffs_ref[...], ((0,), (0,)))


def remove(whole, coeffs, trailing):
    depth, cols = trailing.shape
    n_col, share, _ = whole.shape
    tile = depth // 4
    return pl.pallas_call(
        remove_kernel,
        grid=(depth // tile,),
        out_shape=jax.ShapeDtypeStruct((depth, cols), F32),
        in_specs=[
            pl.BlockSpec((n_col, share, tile), lambda i: (0, 0, i)),
            pl.BlockSpec(coeffs.shape, lambda i: (0, 0)),
            pl.BlockSpec((tile, cols), lambda i: (i, 0)),
        ],
        out_specs=pl.BlockSpec((tile, cols), lambda i: (i, 0)),
        compiler_params=pltpu.CompilerParams(vmem_limit_bytes=56 * 2**20),
    )(whole, coeffs, trailing)


def solution(mesh):
    n_row, n_col = mesh.shape["row"], mesh.shape["col"]

    def shards(panel, trailing):
        factors, blocks, coeffs, whole = chain(panel, trailing, n_row, n_col)
        return factors, blocks, remove(whole, coeffs, trailing)

    return jax.shard_map(
        shards,
        mesh=mesh,
        in_specs=(P("col", "row"), P("row", "col")),
        out_specs=(P("row", None), P("row", "col"), P("row", "col")),
        check_vma=False,
    )
```
